32 devices in a mesh: dp: 16 (over z, y, core), seq: 2 (over x).
Axes of the slice: x: 2, y: 2, z: 4, core: 2. Of those that a mesh axis runs over, the one named last changes fastest.
Arguments:
- qkv: bfloat16 [32, 128, 9216], P('dp', 'seq')
- qkv_tan: bfloat16 [32, 128, 9216], P('dp', 'seq'), may hold values from -6 to 6
- positions: int32 [3, 32, 128], P(None, 'dp', 'seq'), may hold values from 0 to 51, as said below
- step_index: int32 [32], P('dp'), may hold values from 0 to 999
- resid: bfloat16 [32, 128, 2560], P('dp', 'seq'), may hold values from -6 to 6
- resid_tan: bfloat16 [32, 128, 2560], P('dp', 'seq'), may hold values from -6 to 6
- noisy: bfloat16 [32, 128, 2560], P('dp', 'seq'), may hold values from -6 to 6
- noisy_tan: bfloat16 [32, 128, 2560], P('dp', 'seq')
- out_weight: bfloat16 [3072, 2560], P(('seq', 'dp')), may hold values from -0.109375 to 0.109375
- gate_bias: float32 [2560], replicated, may hold values from 0.5 to 1.5
- gate_amp: float32 [2560], replicated, may hold values from 0.2 to 0.8
- gate_freq: float32 [2560], replicated, may hold values from 1 to 6
Outputs:
- d_qkv: bfloat16 [32, 128, 9216], P('dp', 'seq')
- d_weight: float32 [3072, 2560], P(('seq', 'dp'))
The draws below stay inside these ranges and needn't reach their ends.
Inputs may be any that keep to these rules, and one draw needn't show every extreme that they name: positions[0], positions[1], positions[2] are the frame (below 21), row (below 30) and column (below 52) of a token of a latent video grid; the 128 tokens of a clip are consecutive in frame-major order.
All inputs are finite; a program needn't handle non-finite values.
Results may differ from the reference program's by a relative error of at most 0.014.
The reference program's roundings to bfloat16 on the way count: a program that leaves them out, or rounds other values in their place, can miss the bound.
Values may be sent and summed in bfloat16 or wider, within the bound.
A program may use at most 128 MiB of HBM per device.

```python
import math
import jax
import jax.numpy as jnp
from jax import lax

HEADS = 24
HEAD_DIM = 128
DW = 2560
NT = 1000
GRID_F = 21
GRID_H = 30
GRID_W = 52
ATT = 3072
LEN = 128
CLIPS = 32
N_SEQ = 2


def window_starts(key):
    start_count = GRID_F * GRID_H * GRID_W - LEN + 1
    return jax.random.randint(jax.random.fold_in(key, 101), (CLIPS,), 0, start_count)


def grid_place(token):
    frame_size = GRID_H * GRID_W
    rest = token % frame_size
    return jnp.stack([token // frame_size, rest // GRID_W, rest % GRID_W])


def draw_positions(key, part):
    starts = window_starts(key)
    token = starts[:, None] + jnp.arange(LEN, dtype=jnp.int32)[None, :]
    return grid_place(token).astype(jnp.int32)


def draw_qkv(key, part):
    key = jax.random.fold_in(key, 5)
    base_key = jax.random.fold_in(key, 0)
    shape = (CLIPS, LEN, 3 * ATT)
    return jnp.clip(jax.random.normal(base_key, shape, jnp.float32), -6.0, 6.0).astype(jnp.bfloat16)


def draw_noisy_tan(key, part):
    key = jax.random.fold_in(key, 7)
    first_key, row_key, col_key = jax.random.split(key, 3)
    shape = (CLIPS, LEN, DW)
    rise = 1.0 + 2.0 * jnp.arange(LEN, dtype=jnp.float32) / (LEN - 1)
    row_scale = jnp.exp(jax.random.uniform(row_key, (CLIPS, LEN, 1), jnp.float32, 0.0, math.log(3.4)))
    col_scale = 0.3 * jnp.exp(jax.random.uniform(col_key, (1, 1, DW), jnp.float32, 0.0, math.log(10.0)))
    base = jax.random.normal(first_key, shape, jnp.float32)
    return (base * rise[None, :, None] * row_scale * col_scale).astype(jnp.bfloat16)


def place_ends(result, stream_key, smallest, largest):
    longest = result.shape.index(max(result.shape))
    spots = []
    for shift in (0, 1):
        where = [jax.random.randint(jax.random.fold_in(stream_key, axis), (), 0, length) for axis, length in enumerate(result.shape)]
        where[longest] = (where[longest] + shift) % result.shape[longest]
        spots.append(tuple(where))
    return result.at[spots[0]].set(smallest).at[spots[1]].set(largest)


def levels(stream_key, shape, shards, low, high):
    gain, own = 1.0, jax.random.fold_in(stream_key, 6)
    for position, shards_of in shards:
        steps = jnp.exp(jax.random.uniform(jax.random.fold_in(own, position), (shards_of,), jnp.float32, low / len(shards), high / len(shards)))
        gain = gain * jnp.repeat(steps, shape[position] // shards_of).reshape([-1 if axis == position else 1 for axis in range(len(shape))])
    return gain


def normal_values(stream_key, dims, deviation, bound, cuts=(), kind=jnp.bfloat16):
    result = deviation * jax.random.normal(stream_key, dims, jnp.float32)
    if cuts:
        result = result * levels(stream_key, dims, cuts, -0.22, 0.18)
    return jnp.clip(result, -bound, bound).astype(kind)


def setup_inputs(seed: int = 0) -> dict:
    key_list = jax.random.split(jax.random.key(seed), 13)
    qkv = draw_qkv(jax.random.fold_in(key_list[12], 71), 0)
    qkv_tan = normal_values(key_list[1], (CLIPS, LEN, 3 * ATT), 1.0, 6.0, ((0, 16), (1, 2)))
    positions = draw_positions(jax.random.fold_in(key_list[12], 71), 0)
    step_index = place_ends(jax.random.randint(key_list[3], (CLIPS,), 0, NT), jax.random.fold_in(key_list[3], 1), 0, NT - 1).astype(jnp.int32)
    resid = normal_values(key_list[4], (CLIPS, LEN, DW), 1.0, 6.0, ((0, 16), (1, 2)))
    resid_tan = normal_values(key_list[5], (CLIPS, LEN, DW), 1.0, 6.0, ((0, 16), (1, 2)))
    noisy = normal_values(key_list[6], (CLIPS, LEN, DW), 1.0, 6.0, ((0, 16), (1, 2)))
    noisy_tan = draw_noisy_tan(jax.random.fold_in(key_list[12], 71), 0)
    out_weight = normal_values(key_list[8], (ATT, DW), ATT ** -0.5, 0.109375, ((0, 32),))
    gate_bias = jnp.clip(1.0 + 0.1 * jax.random.normal(key_list[9], (DW,), jnp.float32), 0.5, 1.5)
    gate_amp = jnp.clip(jax.random.uniform(key_list[10], (DW,), jnp.float32, 0.2, 0.8), 0.2, 0.8)
    gate_freq = jnp.clip(jnp.exp(jax.random.uniform(key_list[11], (DW,), jnp.float32, math.log(1.0), math.log(6.0))), 1.0, 6.0)
    return dict(qkv=qkv, qkv_tan=qkv_tan, positions=positions, step_index=step_index, resid=resid, resid_tan=resid_tan, noisy=noisy, noisy_tan=noisy_tan, out_weight=out_weight, gate_bias=gate_bias, gate_amp=gate_amp, gate_freq=gate_freq)


def rope_angles(place):
    pairs = HEAD_DIM // 2
    side = pairs // 3
    first = pairs - 2 * side
    index = jnp.arange(pairs, dtype=jnp.int32)
    part = jnp.where(index < first, 0, jnp.where(index < first + side, 1, 2))
    local = index - jnp.where(part == 0, 0, jnp.where(part == 1, first, first + side))
    count = jnp.where(part == 0, first, side)
    freq = jnp.exp(-math.log(10000.0) * local.astype(jnp.float32) / count.astype(jnp.float32))
    spot = place.astype(jnp.float32)
    chosen = jnp.where(part == 0, spot[0][..., None], jnp.where(part == 1, spot[1][..., None], spot[2][..., None]))
    return chosen * freq

def rotate(values, cosine, sine, sign):
    pairs = values.shape[-1] // 2
    first = values[..., :pairs]
    second = values[..., pairs:]
    return jnp.concatenate([first * cosine - sign * second * sine, sign * first * sine + second * cosine], -1)

def group_sum(rows, weight):
    width = ATT // N_SEQ
    terms = jnp.einsum('lgk,gkd->gld', rows.reshape(LEN, N_SEQ, width).astype(jnp.float32), weight.reshape(N_SEQ, width, DW).astype(jnp.float32))
    rounded = lax.optimization_barrier(terms.astype(jnp.bfloat16))
    return lax.optimization_barrier(jnp.sum(rounded.astype(jnp.float32), 0))

def reference(qkv, qkv_tan, positions, step_index, resid, resid_tan, noisy, noisy_tan, out_weight, gate_bias, gate_amp, gate_freq):
    logit_scale = 1.0 / math.sqrt(HEAD_DIM)
    f32 = jnp.float32
    brain_float_half = jnp.bfloat16

    def clip_step(total, item):
        block, block_tan, place, index, res, res_tan, noise, noise_tan = item
        time = 0.05 + 1.47 * (index.astype(f32) + 0.5) / NT
        gate = gate_bias + gate_amp * jnp.sin(gate_freq * time)
        slope = gate_amp * gate_freq * jnp.cos(gate_freq * time)
        angle = rope_angles(place)
        cosine = jnp.cos(angle)[:, None, :]
        sine = jnp.sin(angle)[:, None, :]
        parts = block.reshape(LEN, 3, HEADS, HEAD_DIM)
        parts_tan = block_tan.reshape(LEN, 3, HEADS, HEAD_DIM)
        query_rows = rotate(parts[:, 0].astype(f32), cosine, sine, 1.0).astype(brain_float_half).astype(f32)
        key_rows = rotate(parts[:, 1].astype(f32), cosine, sine, 1.0).astype(brain_float_half).astype(f32)
        value_rows = parts[:, 2].astype(f32)
        query_tangent = rotate(parts_tan[:, 0].astype(f32), cosine, sine, 1.0).astype(brain_float_half).astype(f32)
        key_tangent = rotate(parts_tan[:, 1].astype(f32), cosine, sine, 1.0).astype(brain_float_half).astype(f32)
        value_tangent = parts_tan[:, 2].astype(f32)
        score_matrix = jnp.einsum('tfi,nfi->ftn', query_rows, key_rows) * logit_scale
        probs = jax.nn.softmax(score_matrix, axis=-1)
        low_precision_probs = probs.astype(brain_float_half).astype(f32)
        attention_output = jnp.einsum('asp,paq->saq', low_precision_probs, value_rows).astype(brain_float_half)
        score_tangent = (jnp.einsum('tfi,nfi->ftn', query_tangent, key_rows) + jnp.einsum('tfi,nfi->ftn', query_rows, key_tangent)) * logit_scale
        dprob = probs * (score_tangent - lax.optimization_barrier(jnp.sum(probs * score_tangent, -1, keepdims=True)))
        prob_tangent_grad = dprob.astype(brain_float_half).astype(f32)
        attention_output_tangent = (jnp.einsum('asp,paq->saq', prob_tangent_grad, value_rows) + jnp.einsum('asp,paq->saq', low_precision_probs, value_tangent)).astype(brain_float_half)
        flat = attention_output.reshape(LEN, ATT)
        flat_tan = attention_output_tangent.reshape(LEN, ATT)
        proj = group_sum(flat, out_weight)
        proj_tan = group_sum(flat_tan, out_weight)
        out = res.astype(f32) + gate * proj
        out_tan = res_tan.astype(f32) + gate * proj_tan + slope * proj
        target = -jnp.cos(time) ** 2 * (0.5 * out - noise_tan.astype(f32)) - jnp.cos(time) * jnp.sin(time) * (noise.astype(f32) + 0.5 * out_tan)
        rms = jnp.sqrt(jnp.mean(target * target) + 1e-06)
        cot = -2.0 * target / (rms + 0.1)
        grad_proj = (gate * cot).astype(brain_float_half)
        attention_gradient = jnp.dot(grad_proj, out_weight.T, preferred_element_type=f32).astype(brain_float_half)
        attention_gradient = attention_gradient.reshape(LEN, HEADS, HEAD_DIM).astype(f32)
        value_gradient = jnp.einsum('rby,brs->yrs', low_precision_probs, attention_gradient).astype(brain_float_half)
        probability_gradient = jnp.einsum('tfi,nfi->ftn', attention_gradient, value_rows)
        score_gradient = (probs * (probability_gradient - lax.optimization_barrier(jnp.sum(probs * probability_gradient, -1, keepdims=True))) * logit_scale).astype(brain_float_half).astype(f32)
        query_gradient = jnp.einsum('asp,paq->saq', score_gradient, key_rows).astype(brain_float_half)
        key_gradient = jnp.einsum('rby,brs->yrs', score_gradient, query_rows).astype(brain_float_half)
        back_query = rotate(query_gradient.astype(f32), cosine, sine, -1.0).astype(brain_float_half)
        back_key = rotate(key_gradient.astype(f32), cosine, sine, -1.0).astype(brain_float_half)
        d_block = jnp.stack([back_query, back_key, value_gradient], 1).reshape(LEN, 3 * ATT)
        term = jnp.dot(flat.T, grad_proj, preferred_element_type=f32)
        return (total + term, d_block)
    places = jnp.moveaxis(positions, 1, 0)
    items = (qkv, qkv_tan, places, step_index, resid, resid_tan, noisy, noisy_tan)
    total, d_qkv = lax.scan(clip_step, jnp.zeros((ATT, DW), jnp.float32), items)
    d_weight = total / math.sqrt(CLIPS * LEN)
    return (d_qkv, d_weight)
```

```python
import math

import jax
import jax.numpy as jnp
from jax import lax
from jax.experimental import pallas as pl
from jax.experimental.pallas import tpu as pltpu
from jax.sharding import PartitionSpec as P

HEAD_DIM = 128
NT = 1000
GRID_H = 30
GRID_W = 52
MESH = pl.DeviceIdType.MESH
PLANES, COLUMNS, CORES = 4, 2, 2


def rope_angles(place):
    pairs = HEAD_DIM // 2
    side = pairs // 3
    first = pairs - 2 * side
    index = jnp.arange(pairs, dtype=jnp.int32)
    part = jnp.where(index < first, 0, jnp.where(index < first + side, 1, 2))
    local = index - jnp.where(part == 0, 0, jnp.where(part == 1, first, first + side))
    count = jnp.where(part == 0, first, side)
    freq = jnp.exp(-math.log(10000.0) * local.astype(jnp.float32) / count.astype(jnp.float32))
    spot = place.astype(jnp.float32)
    chosen = jnp.where(
        part == 0, spot[0][..., None], jnp.where(part == 1, spot[1][..., None], spot[2][..., None])
    )
    return chosen * freq


def rotate(values, cosine, sine, sign):
    pairs = values.shape[-1] // 2
    first = values[..., :pairs]
    second = values[..., pairs:]
    return jnp.concatenate(
        [first * cosine - sign * second * sine, sign * first * sine + second * cosine], -1
    )


def body(
    qkv,
    qkv_tan,
    positions,
    step_index,
    resid,
    resid_tan,
    noisy,
    noisy_tan,
    out_weight,
    gate_bias,
    gate_amp,
    gate_freq,
):
    f32 = jnp.float32
    brain_float_half = jnp.bfloat16
    clips, len_dev, triple = qkv.shape
    att = triple // 3
    heads = att // HEAD_DIM
    groups = lax.axis_size("seq")
    heads_dev = heads // groups
    att_dev = att // groups
    seq_len = len_dev * groups
    width = resid.shape[2]
    token_count = lax.axis_size("dp") * clips * seq_len
    logit_scale = 1.0 / math.sqrt(HEAD_DIM)
    angle = rope_angles(positions)
    cosine = jnp.cos(angle)[:, :, None, None, :]
    sine = jnp.sin(angle)[:, :, None, None, :]

    def prepare(block):
        parts = block.reshape(clips, len_dev, 3, heads, HEAD_DIM)
        turned = rotate(parts[:, :, :2].astype(f32), cosine, sine, 1.0).astype(brain_float_half)
        return jnp.concatenate([turned, parts[:, :, 2:]], 2).reshape(clips, len_dev, 3, att)

    mixed, mixed_tan = (
        lax.all_to_all(prepare(qkv), "seq", split_axis=3, concat_axis=1, tiled=True),
        lax.all_to_all(prepare(qkv_tan), "seq", split_axis=3, concat_axis=1, tiled=True),
    )

    def split_heads(block, slot):
        return block[:, :, slot].reshape(clips, seq_len, heads_dev, HEAD_DIM)

    query_rows = split_heads(mixed, 0)
    key_rows = split_heads(mixed, 1)
    value_rows = split_heads(mixed, 2)
    query_tangent = split_heads(mixed_tan, 0)
    key_tangent = split_heads(mixed_tan, 1)
    value_tangent = split_heads(mixed_tan, 2)
    score_matrix = (
        jnp.einsum("clhd,cmhd->chlm", query_rows, key_rows, preferred_element_type=f32)
        * logit_scale
    )
    probs = jax.nn.softmax(score_matrix, axis=-1)
    low_precision_probs = probs.astype(brain_float_half)
    attention_output = jnp.einsum(
        "chlm,cmhd->lchd", low_precision_probs, value_rows, preferred_element_type=f32
    ).astype(brain_float_half)
    score_tangent = (
        jnp.einsum(
            "clhe,cmhe->chlm",
            jnp.concatenate([query_tangent, query_rows], -1),
            jnp.concatenate([key_rows, key_tangent], -1),
            preferred_element_type=f32,
        )
        * logit_scale
    )
    dprob = probs * (score_tangent - jnp.sum(probs * score_tangent, axis=-1, keepdims=True))
    prob_tangent_grad = dprob.astype(brain_float_half)
    attention_output_tangent = jnp.einsum(
        "chlm,cmhd->lchd",
        jnp.concatenate([prob_tangent_grad, low_precision_probs], -1),
        jnp.concatenate([value_rows, value_tangent], 1),
        preferred_element_type=f32,
    ).astype(brain_float_half)
    flat = attention_output.reshape(seq_len, clips, att_dev)
    rows = jnp.stack([attention_output, attention_output_tangent], 1).reshape(
        seq_len, 2, clips, att_dev
    )
    part = rows
    partial_value = jnp.einsum(
        "lsck,kd->lscd",
        part,
        lax.all_gather(out_weight, "dp", axis=0, tiled=True),
        preferred_element_type=f32,
    )
    sums = lax.psum_scatter(
        partial_value.astype(jnp.bfloat16), "seq", scatter_dimension=0, tiled=True
    ).astype(jnp.float32)
    proj = jnp.moveaxis(sums[:, 0], 0, 1)
    proj_tan = jnp.moveaxis(sums[:, 1], 0, 1)
    time = 0.05 + 1.47 * (step_index.astype(f32) + 0.5) / NT
    phase = gate_freq[None, None, :] * time[:, None, None]
    gate = gate_bias + gate_amp * jnp.sin(phase)
    slope = gate_amp * gate_freq * jnp.cos(phase)
    out = resid.astype(f32) + gate * proj
    out_tan = resid_tan.astype(f32) + gate * proj_tan + slope * proj
    cos_sq = (jnp.cos(time) ** 2)[:, None, None]
    cross = (jnp.cos(time) * jnp.sin(time))[:, None, None]
    target = -cos_sq * (0.5 * out - noisy_tan.astype(f32)) - cross * (
        noisy.astype(f32) + 0.5 * out_tan
    )
    local_sq = jnp.sum(target * target, axis=(1, 2))
    total_sq = lax.psum(local_sq, "seq")
    rms = jnp.sqrt(total_sq / (seq_len * width) + 1e-06)[:, None, None]
    cot = -2.0 * target / (rms + 0.1)
    grad_proj = (gate * cot).astype(brain_float_half)
    grad_all = lax.all_gather(grad_proj, "seq", axis=1, tiled=True)
    attention_gradient = jnp.einsum(
        "fev,hv->feh",
        grad_all,
        lax.all_gather(out_weight, "dp", axis=0, tiled=True),
        preferred_element_type=f32,
    ).astype(brain_float_half)
    part = flat
    d_weight = lax.psum_scatter(
        jnp.einsum("lck,cld->kd", part, grad_all, preferred_element_type=f32).astype(jnp.bfloat16),
        "dp",
        scatter_dimension=0,
        tiled=True,
    ).astype(jnp.float32) / math.sqrt(token_count)
    attention_gradient = attention_gradient.reshape(clips, seq_len, heads_dev, HEAD_DIM)
    value_gradient = jnp.einsum(
        "chlm,clhd->cmhd", low_precision_probs, attention_gradient, preferred_element_type=f32
    ).astype(brain_float_half)
    probability_gradient = jnp.einsum(
        "clhd,cmhd->chlm", attention_gradient, value_rows, preferred_element_type=f32
    )
    score_gradient = (
        probs
        * (probability_gradient - jnp.sum(probs * probability_gradient, axis=-1, keepdims=True))
        * logit_scale
    ).astype(brain_float_half)
    query_gradient = jnp.einsum(
        "chlm,cmhd->clhd", score_gradient, key_rows, preferred_element_type=f32
    ).astype(brain_float_half)
    key_gradient = jnp.einsum(
        "chlm,clhd->cmhd", score_gradient, query_rows, preferred_element_type=f32
    ).astype(brain_float_half)
    stacked = jnp.stack([query_gradient, key_gradient, value_gradient], 2).reshape(
        clips, seq_len, 3, att_dev
    )
    back = lax.all_to_all(stacked, "seq", split_axis=1, concat_axis=3, tiled=True)
    parts = back.reshape(clips, len_dev, 3, heads, HEAD_DIM)
    turned = rotate(parts[:, :, :2].astype(f32), cosine, sine, -1.0).astype(brain_float_half)
    d_qkv = jnp.concatenate([turned, parts[:, :, 2:]], 2).reshape(clips, len_dev, 3 * att)
    return (d_qkv, d_weight)


def multiple(value, of):
    return pl.multiple_of(value, of)


def dot(left, right, left_dim, right_dim):
    return lax.dot_general(
        left, right, (((left_dim,), (right_dim,)), ((), ())), preferred_element_type=jnp.float32
    )


def softmax_rows(scores):
    shifted = jnp.exp(scores - jnp.max(scores, axis=-1, keepdims=True))
    return shifted / jnp.sum(shifted, axis=-1, keepdims=True)


def turn(block, cosine, sine):
    wide = block.astype(jnp.float32)
    return (wide * cosine + pltpu.roll(wide, HEAD_DIM // 2, 1) * sine).astype(jnp.bfloat16)


def forward_kernel(
    qkv, qkv_tan, angle, rows, turned, cos_out, sin_out, arrived, send_sem, recv_sem, own_sem
):
    me = lax.axis_index("seq")
    other = 1 - me
    clips, len_dev, triple = qkv.shape
    att = triple // 3
    att_dev = att // 2
    chunks = send_sem.shape[1]
    chunk = att_dev // chunks
    scale = 1.0 / math.sqrt(HEAD_DIM)

    barrier = pltpu.get_barrier_semaphore()
    pl.semaphore_signal(barrier, inc=1, device_id={"seq": other}, device_id_type=MESH)
    pl.semaphore_wait(barrier, 1)

    def copies(clip, part):
        result = []
        for which, source in enumerate((qkv, qkv_tan)):
            for slot in range(3):
                place = arrived.at[
                    clip,
                    which * 3 + slot,
                    pl.ds(multiple(me * len_dev, 64), len_dev),
                    pl.ds(multiple(part * chunk, 128), chunk),
                ]
                theirs = multiple(slot * att + other * att_dev + part * chunk, 128)
                mine = multiple(slot * att + me * att_dev + part * chunk, 128)
                result.append(
                    (
                        pltpu.make_async_remote_copy(
                            src_ref=source.at[clip, :, pl.ds(theirs, chunk)],
                            dst_ref=place,
                            send_sem=send_sem.at[clip, part, which * 3 + slot],
                            recv_sem=recv_sem.at[clip, part, which * 3 + slot],
                            device_id={"seq": other},
                            device_id_type=MESH,
                        ),
                        pltpu.make_async_copy(
                            source.at[clip, :, pl.ds(mine, chunk)],
                            place,
                            own_sem.at[clip, part, which * 3 + slot],
                        ),
                    )
                )
        return result

    def start(step, carry):
        for remote, own in copies(step // chunks, step % chunks):
            remote.start()
            own.start()
        return carry

    lax.fori_loop(0, clips * chunks, start, 0)
    lane = lax.broadcasted_iota(jnp.int32, angle.shape, 2)
    sines = jnp.sin(angle[...])
    cos_out[...] = jnp.cos(angle[...])
    sin_out[...] = jnp.where(lane < HEAD_DIM // 2, -sines, sines)

    def attend(step, carry):
        clip, part = step // chunks, step % chunks
        for remote, own in copies(clip, part):
            remote.wait()
            own.wait()
        cosine, sine = cos_out[clip], sin_out[clip]
        for head in range(chunk // HEAD_DIM):
            at = pl.ds(multiple(part * chunk + head * HEAD_DIM, 128), HEAD_DIM)
            query = turn(arrived[clip, 0, :, at], cosine, sine)
            key = turn(arrived[clip, 1, :, at], cosine, sine)
            value = arrived[clip, 2, :, at]
            query_tan = turn(arrived[clip, 3, :, at], cosine, sine)
            key_tan = turn(arrived[clip, 4, :, at], cosine, sine)
            value_tan = arrived[clip, 5, :, at]
            turned[clip, 0, :, at] = query
            turned[clip, 1, :, at] = key
            turned[clip, 2, :, at] = value
            probs = softmax_rows(dot(query, key, 1, 1) * scale)
            low = probs.astype(jnp.bfloat16)
            length = low.shape[0]
            rows[clip, :length, at] = dot(low, value, 1, 0).astype(jnp.bfloat16)
            dscore = scale * dot(
                jnp.concatenate([query_tan, query], 1), jnp.concatenate([key, key_tan], 1), 1, 1
            )
            dprob = probs * (dscore - jnp.sum(probs * dscore, axis=-1, keepdims=True))
            both = jnp.concatenate([dprob.astype(jnp.bfloat16), low], 1)
            rows[clip, length:, at] = dot(
                both, jnp.concatenate([value, value_tan], 0), 1, 0
            ).astype(jnp.bfloat16)
        return carry

    lax.fori_loop(0, clips * chunks, attend, 0)


def backward_kernel(
    weight,
    rows,
    turned,
    known,
    coef,
    cos_tab,
    sin_tab,
    d_qkv,
    d_weight,
    total,
    outgoing,
    incoming,
    grad_proj,
    grads,
    partial,
    from_core,
    from_column,
    from_plane,
    swap_send,
    swap_recv,
    grad_send,
    grad_recv,
    grad_own,
    core_send,
    core_recv,
    column_send,
    column_recv,
    plane_send,
    plane_recv,
):
    f32, half = jnp.float32, jnp.bfloat16
    me = lax.axis_index("seq")
    other = 1 - me
    place = lax.axis_index("dp")
    plane, column, core = place // (COLUMNS * CORES), (place // CORES) % COLUMNS, place % CORES

    def index(at_plane, at_column, at_core):
        return (at_plane * COLUMNS + at_column) * CORES + at_core

    clips, length, width = total.shape
    att_dev = weight.shape[0]
    len_dev = length // 2
    att = att_dev * 2
    scale = 1.0 / math.sqrt(HEAD_DIM)
    block = d_weight.shape[0]
    tiles = swap_send.shape[1]
    tile = width // tiles
    chunks = grad_send.shape[1]
    chunk = att_dev // chunks
    token_count = lax.axis_size("dp") * clips * length

    barrier = pltpu.get_barrier_semaphore()
    pl.semaphore_signal(barrier, inc=1, device_id={"seq": other}, device_id_type=MESH)
    partners = [index(plane, column, 1 - core), index(plane, 1 - column, core)]
    partners += [index((plane + 1 + step) % PLANES, column, core) for step in range(PLANES - 1)]
    for partner in partners:
        pl.semaphore_signal(barrier, inc=1, device_id={"dp": partner}, device_id_type=MESH)
    pl.semaphore_wait(barrier, 1 + len(partners))

    def swap(clip, part):
        at = pl.ds(multiple(part * tile, 128), tile)
        return pltpu.make_async_remote_copy(
            src_ref=outgoing.at[clip, :, at],
            dst_ref=incoming.at[clip, :, at],
            send_sem=swap_send.at[clip, part],
            recv_sem=swap_recv.at[clip, part],
            device_id={"seq": other},
            device_id_type=MESH,
        )

    def project(step, carry):
        clip, part = step // tiles, step % tiles
        at = pl.ds(multiple(part * tile, 128), tile)
        both = dot(rows[clip], weight[:, at], 1, 0).astype(half).astype(f32)
        total[clip, :, at] = (
            coef[clip, 0:1, at] * both[:length] + coef[clip, 1:2, at] * both[length:]
        )
        mine = pl.ds(multiple(me * len_dev, 64), len_dev)
        total[clip, mine, at] = total[clip, mine, at] + known[clip, :, at]
        outgoing[clip, :, at] = total[clip, :, at].astype(half)
        swap(clip, part).start()
        return carry

    lax.fori_loop(0, clips * tiles, project, 0)

    strip = 16

    def differentiate(clip):
        for part in range(tiles):
            swap(clip, part).wait()

        def add(step, squares):
            at = pl.ds(multiple(step * strip, strip), strip)
            target = total[clip, at, :] + incoming[clip, at, :].astype(f32)
            total[clip, at, :] = target
            return squares + jnp.sum(target * target, axis=0, keepdims=True)

        squares = lax.fori_loop(0, length // strip, add, jnp.zeros((1, width), f32))
        mean = jnp.sum(squares, axis=1, keepdims=True) / (length * width)
        factor = -2.0 / (jnp.sqrt(mean + 1e-06) + 0.1)

        def scaled(step, carry):
            at = pl.ds(multiple(step * strip, strip), strip)
            cot = total[clip, at, :] * factor
            grad_proj[pl.ds(multiple(clip * length + step * strip, strip), strip), :] = (
                coef[clip, 2:3, :] * cot
            ).astype(half)
            return carry

        lax.fori_loop(0, length // strip, scaled, 0)

    def grad_copies(clip, part):
        result = []
        for slot in range(3):
            at = pl.ds(multiple(part * chunk, 128), chunk)
            out_at = pl.ds(multiple(slot * att + me * att_dev + part * chunk, 128), chunk)
            result.append(
                (
                    pltpu.make_async_remote_copy(
                        src_ref=grads.at[clip, slot, pl.ds(multiple(other * len_dev, 64), len_dev), at],
                        dst_ref=d_qkv.at[clip, :, out_at],
                        send_sem=grad_send.at[clip, part, slot],
                        recv_sem=grad_recv.at[clip, part, slot],
                        device_id={"seq": other},
                        device_id_type=MESH,
                    ),
                    pltpu.make_async_copy(
                        grads.at[clip, slot, pl.ds(multiple(me * len_dev, 64), len_dev), at],
                        d_qkv.at[clip, :, out_at],
                        grad_own.at[clip, part, slot],
                    ),
                )
            )
        return result

    def attend_back(clip, part):
        cosine, sine = cos_tab[clip], sin_tab[clip]
        grad_att = dot(
            grad_proj[pl.ds(multiple(clip * length, length), length), :],
            weight[pl.ds(multiple(part * chunk, 128), chunk), :],
            1,
            1,
        ).astype(half)
        for head in range(chunk // HEAD_DIM):
            at = pl.ds(multiple(part * chunk + head * HEAD_DIM, 128), HEAD_DIM)
            query, key, value = turned[clip, 0, :, at], turned[clip, 1, :, at], turned[clip, 2, :, at]
            upper = grad_att[:, head * HEAD_DIM : (head + 1) * HEAD_DIM]
            probs = softmax_rows(dot(query, key, 1, 1) * scale)
            grad_value = dot(probs.astype(half), upper, 0, 0).astype(half)
            grad_prob = dot(upper, value, 1, 1)
            grad_score = (
                probs * (grad_prob - jnp.sum(probs * grad_prob, axis=-1, keepdims=True)) * scale
            ).astype(half)
            grad_query = dot(grad_score, key, 1, 0).astype(half)
            grad_key = dot(grad_score, query, 0, 0).astype(half)
            grads[clip, 0, :, at] = turn(grad_query, cosine, -sine)
            grads[clip, 1, :, at] = turn(grad_key, cosine, -sine)
            grads[clip, 2, :, at] = grad_value
        for remote, own in grad_copies(clip, part):
            remote.start()
            own.start()

    def back(clip):
        def step(part, carry):
            attend_back(clip, part)
            return carry

        lax.fori_loop(0, chunks, step, 0)

    def block_at(at_plane, at_column, at_core):
        return pl.ds(multiple(index(at_plane, at_column, at_core) * block, 32), block)

    def to_core(step, at_column):
        to_plane = (plane + 1 + step) % PLANES
        return pltpu.make_async_remote_copy(
            src_ref=partial.at[block_at(to_plane, at_column, 1 - core), :],
            dst_ref=from_core.at[step, at_column],
            send_sem=core_send.at[step, at_column],
            recv_sem=core_recv.at[step, at_column],
            device_id={"dp": index(plane, column, 1 - core)},
            device_id_type=MESH,
        )

    def to_column(step):
        to_plane = (plane + 1 + step) % PLANES
        return pltpu.make_async_remote_copy(
            src_ref=partial.at[block_at(to_plane, 1 - column, core), :],
            dst_ref=from_column.at[step],
            send_sem=column_send.at[step],
            recv_sem=column_recv.at[step],
            device_id={"dp": index(plane, 1 - column, core)},
            device_id_type=MESH,
        )

    def to_plane_copy(step):
        to_plane = (plane + 1 + step) % PLANES
        return pltpu.make_async_remote_copy(
            src_ref=partial.at[block_at(to_plane, column, core), :],
            dst_ref=from_plane.at[step],
            send_sem=plane_send.at[step],
            recv_sem=plane_recv.at[step],
            device_id={"dp": index(to_plane, column, core)},
            device_id_type=MESH,
        )

    piece = COLUMNS * CORES * block

    def weight_piece(step, carry):
        to_plane = (plane + 1 + step) % PLANES
        cols = pl.ds(multiple(to_plane * piece, 128), piece)
        left = jnp.concatenate([rows[clip, :length, cols] for clip in range(clips)], 0)

        def one(part, inner):
            at = pl.ds(multiple(part * tile, 128), tile)
            partial[pl.ds(multiple(to_plane * piece, 128), piece), at] = dot(
                left, grad_proj[:, at], 0, 0
            ).astype(half)
            return inner

        lax.fori_loop(0, tiles, one, 0)
        to_core(step, 0).start()
        to_core(step, 1).start()
        return carry

    def add_rows(row, source):
        for lower in range(0, block, 32):
            at = pl.ds(multiple(row * block + lower, 32), 32)
            partial[at, :] = (
                partial[at, :].astype(f32) + source[lower : lower + 32, :].astype(f32)
            ).astype(half)

    def core_stage(step, carry):
        to_plane = (plane + 1 + step) % PLANES
        to_core(step, 0).wait()
        to_core(step, 1).wait()
        for at_column in range(COLUMNS):
            add_rows(index(to_plane, at_column, core), from_core.at[step, at_column])
        to_column(step).start()
        return carry

    def column_stage(step):
        to_plane = (plane + 1 + step) % PLANES
        to_column(step).wait()
        add_rows(index(to_plane, column, core), from_column.at[step])

    def send_plane(step, carry):
        column_stage(step)
        to_plane_copy(step).start()
        return carry

    differentiate(0)
    back(0)
    for clip in range(1, clips):
        differentiate(clip)
    lax.fori_loop(0, PLANES, weight_piece, 0)
    lax.fori_loop(0, PLANES, core_stage, 0)
    for clip in range(1, clips):
        for part in range(chunks):
            attend_back(clip, part)
            if clip == 1:
                send_plane(part, 0)
    column_stage(PLANES - 1)
    for step in range(PLANES - 1):
        to_plane_copy(step).wait()
    root = 1.0 / math.sqrt(token_count)
    for lower in range(0, block, 32):
        own = multiple(index(plane, column, core) * block + lower, 32)
        value = partial[pl.ds(own, 32), :].astype(f32)
        for step in range(PLANES - 1):
            value = value + from_plane[step, lower : lower + 32, :].astype(f32)
        d_weight[lower : lower + 32, :] = value * root

    def finish(step, carry):
        for remote, own in grad_copies(step // chunks, step % chunks):
            remote.wait()
            own.wait()
        return carry

    lax.fori_loop(0, clips * chunks, finish, 0)


def whole_positions(positions, seq_len, len_dev):
    first = (positions[0, :, 0] * GRID_H + positions[1, :, 0]) * GRID_W + positions[2, :, 0]
    first = first - lax.axis_index("seq") * len_dev
    token = first[:, None] + jnp.arange(seq_len, dtype=jnp.int32)[None, :]
    rest = token % (GRID_H * GRID_W)
    return jnp.stack([token // (GRID_H * GRID_W), rest // GRID_W, rest % GRID_W])


def body_pair(
    qkv,
    qkv_tan,
    positions,
    step_index,
    resid,
    resid_tan,
    noisy,
    noisy_tan,
    out_weight,
    gate_bias,
    gate_amp,
    gate_freq,
):
    f32, half = jnp.float32, jnp.bfloat16
    clips, len_dev, triple = qkv.shape
    att_dev = triple // 6
    seq_len = len_dev * 2
    width = resid.shape[2]
    block = out_weight.shape[0]
    angle = rope_angles(whole_positions(positions, seq_len, len_dev))
    angle = jnp.concatenate([angle, angle], -1)
    weight = lax.all_gather(out_weight, "dp", axis=0, tiled=True)
    vmem = pl.BlockSpec(memory_space=pltpu.VMEM)
    hbm = pl.BlockSpec(memory_space=pl.ANY)
    chunks = 3
    dma = pltpu.SemaphoreType.DMA
    rows, turned, cos_tab, sin_tab = pl.pallas_call(
        forward_kernel,
        out_shape=(
            jax.ShapeDtypeStruct((clips, 2 * seq_len, att_dev), half),
            jax.ShapeDtypeStruct((clips, 3, seq_len, att_dev), half),
            jax.ShapeDtypeStruct((clips, seq_len, HEAD_DIM), f32),
            jax.ShapeDtypeStruct((clips, seq_len, HEAD_DIM), f32),
        ),
        in_specs=[hbm, hbm, vmem],
        out_specs=(vmem, vmem, vmem, vmem),
        scratch_shapes=[
            pltpu.VMEM((clips, 6, seq_len, att_dev), half),
            dma((clips, chunks, 6)),
            dma((clips, chunks, 6)),
            dma((clips, chunks, 6)),
        ],
        compiler_params=pltpu.CompilerParams(
            collective_id=0, has_side_effects=True, vmem_limit_bytes=32 * 2**20
        ),
    )(qkv, qkv_tan, angle)

    time = 0.05 + 1.47 * (step_index.astype(f32) + 0.5) / NT
    phase = gate_freq[None, :] * time[:, None]
    gate = gate_bias + gate_amp * jnp.sin(phase)
    slope = gate_amp * gate_freq * jnp.cos(phase)
    cos_sq = (jnp.cos(time) ** 2)[:, None]
    cross = (jnp.cos(time) * jnp.sin(time))[:, None]
    known = -cos_sq[:, :, None] * (0.5 * resid.astype(f32) - noisy_tan.astype(f32)) - cross[
        :, :, None
    ] * (noisy.astype(f32) + 0.5 * resid_tan.astype(f32))
    coef = jnp.stack(
        [-0.5 * (cos_sq * gate + cross * slope), -0.5 * cross * gate, gate], axis=1
    )
    tiles = 5
    return pl.pallas_call(
        backward_kernel,
        out_shape=(
            jax.ShapeDtypeStruct((clips, len_dev, triple), half),
            jax.ShapeDtypeStruct((block, width), f32),
        ),
        in_specs=[vmem] * 7,
        out_specs=(hbm, vmem),
        scratch_shapes=[
            pltpu.VMEM((clips, seq_len, width), f32),
            pltpu.VMEM((clips, seq_len, width), half),
            pltpu.VMEM((clips, seq_len, width), half),
            pltpu.VMEM((clips * seq_len, width), half),
            pltpu.VMEM((clips, 3, seq_len, att_dev), half),
            pltpu.VMEM((att_dev, width), half),
            pltpu.VMEM((PLANES, COLUMNS, block, width), half),
            pltpu.VMEM((PLANES, block, width), half),
            pltpu.VMEM((PLANES - 1, block, width), half),
            dma((clips, tiles)),
            dma((clips, tiles)),
            dma((clips, chunks, 3)),
            dma((clips, chunks, 3)),
            dma((clips, chunks, 3)),
            dma((PLANES, COLUMNS)),
            dma((PLANES, COLUMNS)),
            dma((PLANES,)),
            dma((PLANES,)),
            dma((PLANES - 1,)),
            dma((PLANES - 1,)),
        ],
        compiler_params=pltpu.CompilerParams(
            collective_id=1, has_side_effects=True, vmem_limit_bytes=58 * 2**20
        ),
    )(weight, rows, turned, known, coef, cos_tab, sin_tab)


def solution(mesh):
    placed = (
        P("dp", "seq", None),
        P("dp", "seq", None),
        P(None, "dp", "seq"),
        P("dp"),
        P("dp", "seq", None),
        P("dp", "seq", None),
        P("dp", "seq", None),
        P("dp", "seq", None),
        P(("seq", "dp"), None),
        P(),
        P(),
        P(),
    )
    fits = mesh.shape["dp"] == PLANES * COLUMNS * CORES and mesh.shape["seq"] == 2
    return jax.shard_map(
        body_pair if fits else body,
        mesh=mesh,
        in_specs=placed,
        out_specs=(P("dp", "seq", None), P(("seq", "dp"), None)),
        check_vma=False,
    )
```

```python
import math

import jax
import jax.numpy as jnp
from jax import lax
from jax.experimental import pallas as pl
from jax.experimental.pallas import tpu as pltpu
from jax.sharding import PartitionSpec as P

HEAD_DIM = 128
NT = 1000
GRID_H = 30
GRID_W = 52
MESH = pl.DeviceIdType.MESH
PLANES, COLUMNS, CORES = 4, 2, 2


def rope_angles(place):
    pairs = HEAD_DIM // 2
    side = pairs // 3
    first = pairs - 2 * side
    index = jnp.arange(pairs, dtype=jnp.int32)
    part = jnp.where(index < first, 0, jnp.where(index < first + side, 1, 2))
    local = index - jnp.where(part == 0, 0, jnp.where(part == 1, first, first + side))
    count = jnp.where(part == 0, first, side)
    freq = jnp.exp(-math.log(10000.0) * local.astype(jnp.float32) / count.astype(jnp.float32))
    spot = place.astype(jnp.float32)
    chosen = jnp.where(
        part == 0, spot[0][..., None], jnp.where(part == 1, spot[1][..., None], spot[2][..., None])
    )
    return chosen * freq


def rotate(values, cosine, sine, sign):
    pairs = values.shape[-1] // 2
    first = values[..., :pairs]
    second = values[..., pairs:]
    return jnp.concatenate(
        [first * cosine - sign * second * sine, sign * first * sine + second * cosine], -1
    )


def body(
    qkv,
    qkv_tan,
    positions,
    step_index,
    resid,
    resid_tan,
    noisy,
    noisy_tan,
    out_weight,
    gate_bias,
    gate_amp,
    gate_freq,
):
    f32 = jnp.float32
    brain_float_half = jnp.bfloat16
    clips, len_dev, triple = qkv.shape
    att = triple // 3
    heads = att // HEAD_DIM
    groups = lax.axis_size("seq")
    heads_dev = heads // groups
    att_dev = att // groups
    seq_len = len_dev * groups
    width = resid.shape[2]
    token_count = lax.axis_size("dp") * clips * seq_len
    logit_scale = 1.0 / math.sqrt(HEAD_DIM)
    angle = rope_angles(positions)
    cosine = jnp.cos(angle)[:, :, None, None, :]
    sine = jnp.sin(angle)[:, :, None, None, :]

    def prepare(block):
        parts = block.reshape(clips, len_dev, 3, heads, HEAD_DIM)
        turned = rotate(parts[:, :, :2].astype(f32), cosine, sine, 1.0).astype(brain_float_half)
        return jnp.concatenate([turned, parts[:, :, 2:]], 2).reshape(clips, len_dev, 3, att)

    mixed, mixed_tan = (
        lax.all_to_all(prepare(qkv), "seq", split_axis=3, concat_axis=1, tiled=True),
        lax.all_to_all(prepare(qkv_tan), "seq", split_axis=3, concat_axis=1, tiled=True),
    )

    def split_heads(block, slot):
        return block[:, :, slot].reshape(clips, seq_len, heads_dev, HEAD_DIM)

    query_rows = split_heads(mixed, 0)
    key_rows = split_heads(mixed, 1)
    value_rows = split_heads(mixed, 2)
    query_tangent = split_heads(mixed_tan, 0)
    key_tangent = split_heads(mixed_tan, 1)
    value_tangent = split_heads(mixed_tan, 2)
    score_matrix = (
        jnp.einsum("clhd,cmhd->chlm", query_rows, key_rows, preferred_element_type=f32)
        * logit_scale
    )
    probs = jax.nn.softmax(score_matrix, axis=-1)
    low_precision_probs = probs.astype(brain_float_half)
    attention_output = jnp.einsum(
        "chlm,cmhd->lchd", low_precision_probs, value_rows, preferred_element_type=f32
    ).astype(brain_float_half)
    score_tangent = (
        jnp.einsum(
            "clhe,cmhe->chlm",
            jnp.concatenate([query_tangent, query_rows], -1),
            jnp.concatenate([key_rows, key_tangent], -1),
            preferred_element_type=f32,
        )
        * logit_scale
    )
    dprob = probs * (score_tangent - jnp.sum(probs * score_tangent, axis=-1, keepdims=True))
    prob_tangent_grad = dprob.astype(brain_float_half)
    attention_output_tangent = jnp.einsum(
        "chlm,cmhd->lchd",
        jnp.concatenate([prob_tangent_grad, low_precision_probs], -1),
        jnp.concatenate([value_rows, value_tangent], 1),
        preferred_element_type=f32,
    ).astype(brain_float_half)
    flat = attention_output.reshape(seq_len, clips, att_dev)
    rows = jnp.stack([attention_output, attention_output_tangent], 1).reshape(
        seq_len, 2, clips, att_dev
    )
    part = rows
    partial_value = jnp.einsum(
        "lsck,kd->lscd",
        part,
        lax.all_gather(out_weight, "dp", axis=0, tiled=True),
        preferred_element_type=f32,
    )
    sums = lax.psum_scatter(
        partial_value.astype(jnp.bfloat16), "seq", scatter_dimension=0, tiled=True
    ).astype(jnp.float32)
    proj = jnp.moveaxis(sums[:, 0], 0, 1)
    proj_tan = jnp.moveaxis(sums[:, 1], 0, 1)
    time = 0.05 + 1.47 * (step_index.astype(f32) + 0.5) / NT
    phase = gate_freq[None, None, :] * time[:, None, None]
    gate = gate_bias + gate_amp * jnp.sin(phase)
    slope = gate_amp * gate_freq * jnp.cos(phase)
    out = resid.astype(f32) + gate * proj
    out_tan = resid_tan.astype(f32) + gate * proj_tan + slope * proj
    cos_sq = (jnp.cos(time) ** 2)[:, None, None]
    cross = (jnp.cos(time) * jnp.sin(time))[:, None, None]
    target = -cos_sq * (0.5 * out - noisy_tan.astype(f32)) - cross * (
        noisy.astype(f32) + 0.5 * out_tan
    )
    local_sq = jnp.sum(target * target, axis=(1, 2))
    total_sq = lax.psum(local_sq, "seq")
    rms = jnp.sqrt(total_sq / (seq_len * width) + 1e-06)[:, None, None]
    cot = -2.0 * target / (rms + 0.1)
    grad_proj = (gate * cot).astype(brain_float_half)
    grad_all = lax.all_gather(grad_proj, "seq", axis=1, tiled=True)
    attention_gradient = jnp.einsum(
        "fev,hv->feh",
        grad_all,
        lax.all_gather(out_weight, "dp", axis=0, tiled=True),
        preferred_element_type=f32,
    ).astype(brain_float_half)
    part = flat
    d_weight = lax.psum_scatter(
        jnp.einsum("lck,cld->kd", part, grad_all, preferred_element_type=f32).astype(jnp.bfloat16),
        "dp",
        scatter_dimension=0,
        tiled=True,
    ).astype(jnp.float32) / math.sqrt(token_count)
    attention_gradient = attention_gradient.reshape(clips, seq_len, heads_dev, HEAD_DIM)
    value_gradient = jnp.einsum(
        "chlm,clhd->cmhd", low_precision_probs, attention_gradient, preferred_element_type=f32
    ).astype(brain_float_half)
    probability_gradient = jnp.einsum(
        "clhd,cmhd->chlm", attention_gradient, value_rows, preferred_element_type=f32
    )
    score_gradient = (
        probs
        * (probability_gradient - jnp.sum(probs * probability_gradient, axis=-1, keepdims=True))
        * logit_scale
    ).astype(brain_float_half)
    query_gradient = jnp.einsum(
        "chlm,cmhd->clhd", score_gradient, key_rows, preferred_element_type=f32
    ).astype(brain_float_half)
    key_gradient = jnp.einsum(
        "chlm,clhd->cmhd", score_gradient, query_rows, preferred_element_type=f32
    ).astype(brain_float_half)
    stacked = jnp.stack([query_gradient, key_gradient, value_gradient], 2).reshape(
        clips, seq_len, 3, att_dev
    )
    back = lax.all_to_all(stacked, "seq", split_axis=1, concat_axis=3, tiled=True)
    parts = back.reshape(clips, len_dev, 3, heads, HEAD_DIM)
    turned = rotate(parts[:, :, :2].astype(f32), cosine, sine, -1.0).astype(brain_float_half)
    d_qkv = jnp.concatenate([turned, parts[:, :, 2:]], 2).reshape(clips, len_dev, 3 * att)
    return (d_qkv, d_weight)


def multiple(value, of):
    return pl.multiple_of(value, of)


def dot(left, right, left_dim, right_dim):
    return lax.dot_general(
        left, right, (((left_dim,), (right_dim,)), ((), ())), preferred_element_type=jnp.float32
    )


def softmax_rows(scores):
    shifted = jnp.exp(scores - jnp.max(scores, axis=-1, keepdims=True))
    return shifted / jnp.sum(shifted, axis=-1, keepdims=True)


def turn(block, cosine, sine):
    wide = block.astype(jnp.float32)
    return (wide * cosine + pltpu.roll(wide, HEAD_DIM // 2, 1) * sine).astype(jnp.bfloat16)


def step_kernel(
    qkv,
    qkv_tan,
    angle,
    own_weight,
    known,
    coef,
    d_qkv,
    d_weight,
    arrived,
    rows,
    cos_tab,
    sin_tab,
    weight,
    total,
    outgoing,
    incoming,
    grad_proj,
    grads,
    partial,
    from_core,
    from_column,
    from_plane,
    send_sem,
    recv_sem,
    own_sem,
    spread_send,
    spread_recv,
    swap_send,
    swap_recv,
    grad_send,
    grad_recv,
    grad_own,
    core_send,
    core_recv,
    column_send,
    column_recv,
    plane_send,
    plane_recv,
):
    f32, half = jnp.float32, jnp.bfloat16
    me = lax.axis_index("seq")
    other = 1 - me
    place = lax.axis_index("dp")
    plane, column, core = place // (COLUMNS * CORES), (place // CORES) % COLUMNS, place % CORES

    def index(at_plane, at_column, at_core):
        return (at_plane * COLUMNS + at_column) * CORES + at_core

    clips, length, width = total.shape
    att_dev = weight.shape[0]
    len_dev = length // 2
    att = att_dev * 2
    scale = 1.0 / math.sqrt(HEAD_DIM)
    block = d_weight.shape[0]
    tiles = swap_send.shape[1]
    tile = width // tiles
    chunks = grad_send.shape[1]
    chunk = att_dev // chunks
    token_count = lax.axis_size("dp") * clips * length

    barrier = pltpu.get_barrier_semaphore()
    pl.semaphore_signal(barrier, inc=1, device_id={"seq": other}, device_id_type=MESH)
    partners = [index(plane, column, 1 - core), index(plane, 1 - column, core)]
    partners += [index((plane + 1 + step) % PLANES, column, core) for step in range(PLANES - 1)]
    for partner in partners:
        pl.semaphore_signal(barrier, inc=1, device_id={"dp": partner}, device_id_type=MESH)
    pl.semaphore_wait(barrier, 1 + len(partners))

    def block_at(at_plane, at_column, at_core):
        return pl.ds(multiple(index(at_plane, at_column, at_core) * block, 32), block)

    def spread(at_plane, at_column, slot, partner, own=False):
        there = block_at(at_plane, at_column, core)
        return pltpu.make_async_remote_copy(
            src_ref=own_weight if own else weight.at[there, :],
            dst_ref=weight.at[there, :],
            send_sem=spread_send.at[slot],
            recv_sem=spread_recv.at[slot],
            device_id={"dp": partner},
            device_id_type=MESH,
        )

    sibling, beside = index(plane, column, 1 - core), index(plane, 1 - column, core)

    def to_planes(step):
        return spread(
            plane, column, step, index((plane + 1 + step) % PLANES, column, core), own=True
        )

    def behind(step):
        return (plane + PLANES - step) % PLANES

    def to_beside(step):
        return spread(behind(step), column, PLANES - 1 + step, beside, own=step == 0)

    def to_sibling(step, swapped):
        at_column = 1 - column if swapped else column
        return spread(
            behind(step),
            at_column,
            2 * PLANES - 1 + 2 * step + swapped,
            sibling,
            own=step == 0 and not swapped,
        )

    for step in range(PLANES - 1):
        to_planes(step).start()
    to_beside(0).start()
    to_sibling(0, 0).start()

    def copies(clip, part):
        result = []
        for which, source in enumerate((qkv, qkv_tan)):
            for slot in range(3):
                place = arrived.at[
                    clip,
                    which * 3 + slot,
                    pl.ds(multiple(me * len_dev, 64), len_dev),
                    pl.ds(multiple(part * chunk, 128), chunk),
                ]
                theirs = multiple(slot * att + other * att_dev + part * chunk, 128)
                mine = multiple(slot * att + me * att_dev + part * chunk, 128)
                result.append(
                    (
                        pltpu.make_async_remote_copy(
                            src_ref=source.at[clip, :, pl.ds(theirs, chunk)],
                            dst_ref=place,
                            send_sem=send_sem.at[clip, part, which * 3 + slot],
                            recv_sem=recv_sem.at[clip, part, which * 3 + slot],
                            device_id={"seq": other},
                            device_id_type=MESH,
                        ),
                        pltpu.make_async_copy(
                            source.at[clip, :, pl.ds(mine, chunk)],
                            place,
                            own_sem.at[clip, part, which * 3 + slot],
                        ),
                    )
                )
        return result

    def start(step, carry):
        for remote, own in copies(step // chunks, step % chunks):
            remote.start()
            own.start()
        return carry

    lax.fori_loop(0, clips * chunks, start, 0)
    weight[block_at(plane, column, core), :] = own_weight[...]
    lane = lax.broadcasted_iota(jnp.int32, angle.shape, 2)
    sines = jnp.sin(angle[...])
    cos_tab[...] = jnp.cos(angle[...])
    sin_tab[...] = jnp.where(lane < HEAD_DIM // 2, -sines, sines)

    def attend(step, carry):
        clip, part = step // chunks, step % chunks
        for remote, own in copies(clip, part):
            remote.wait()
            own.wait()
        cosine, sine = cos_tab[clip], sin_tab[clip]
        for head in range(chunk // HEAD_DIM):
            at = pl.ds(multiple(part * chunk + head * HEAD_DIM, 128), HEAD_DIM)
            query = turn(arrived[clip, 0, :, at], cosine, sine)
            key = turn(arrived[clip, 1, :, at], cosine, sine)
            value = arrived[clip, 2, :, at]
            query_tan = turn(arrived[clip, 3, :, at], cosine, sine)
            key_tan = turn(arrived[clip, 4, :, at], cosine, sine)
            value_tan = arrived[clip, 5, :, at]
            arrived[clip, 0, :, at] = query
            arrived[clip, 1, :, at] = key
            probs = softmax_rows(dot(query, key, 1, 1) * scale)
            low = probs.astype(half)
            rows[clip, :length, at] = dot(low, value, 1, 0).astype(half)
            dscore = scale * dot(
                jnp.concatenate([query_tan, query], 1), jnp.concatenate([key, key_tan], 1), 1, 1
            )
            dprob = probs * (dscore - jnp.sum(probs * dscore, axis=-1, keepdims=True))
            both = jnp.concatenate([dprob.astype(half), low], 1)
            rows[clip, length:, at] = dot(
                both, jnp.concatenate([value, value_tan], 0), 1, 0
            ).astype(half)
        return carry

    lax.fori_loop(0, 2, attend, 0)
    to_planes(0).wait_recv()
    to_beside(1).start()
    to_sibling(1, 0).start()
    to_beside(0).wait_recv()
    to_sibling(0, 1).start()
    lax.fori_loop(2, 3, attend, 0)
    to_planes(1).wait_recv()
    to_beside(2).start()
    to_sibling(2, 0).start()
    lax.fori_loop(3, 4, attend, 0)
    to_planes(2).wait_recv()
    to_beside(3).start()
    to_sibling(3, 0).start()
    to_beside(1).wait_recv()
    to_sibling(1, 1).start()
    lax.fori_loop(4, 5, attend, 0)
    to_beside(2).wait_recv()
    to_sibling(2, 1).start()
    lax.fori_loop(5, clips * chunks, attend, 0)
    to_beside(3).wait_recv()
    to_sibling(3, 1).start()
    for step in range(PLANES - 1):
        to_planes(step).wait_send()
    for step in range(PLANES):
        to_beside(step).wait_send()
        to_sibling(step, 0).wait()
        to_sibling(step, 1).wait()

    def swap(clip, part):
        at = pl.ds(multiple(part * tile, 128), tile)
        return pltpu.make_async_remote_copy(
            src_ref=outgoing.at[clip, :, at],
            dst_ref=incoming.at[clip, :, at],
            send_sem=swap_send.at[clip, part],
            recv_sem=swap_recv.at[clip, part],
            device_id={"seq": other},
            device_id_type=MESH,
        )

    def project(step, carry):
        clip, part = step // tiles, step % tiles
        at = pl.ds(multiple(part * tile, 128), tile)
        both = dot(rows[clip], weight[:, at], 1, 0).astype(half).astype(f32)
        total[clip, :, at] = (
            coef[clip, 0:1, at] * both[:length] + coef[clip, 1:2, at] * both[length:]
        )
        mine = pl.ds(multiple(me * len_dev, 64), len_dev)
        total[clip, mine, at] = total[clip, mine, at] + known[clip, :, at]
        outgoing[clip, :, at] = total[clip, :, at].astype(half)
        swap(clip, part).start()
        return carry

    lax.fori_loop(0, clips * tiles, project, 0)

    strip = 16

    def differentiate(clip):
        for part in range(tiles):
            swap(clip, part).wait()

        def add(step, squares):
            at = pl.ds(multiple(step * strip, strip), strip)
            target = total[clip, at, :] + incoming[clip, at, :].astype(f32)
            total[clip, at, :] = target
            return squares + jnp.sum(target * target, axis=0, keepdims=True)

        squares = lax.fori_loop(0, length // strip, add, jnp.zeros((1, width), f32))
        mean = jnp.sum(squares, axis=1, keepdims=True) / (length * width)
        factor = -2.0 / (jnp.sqrt(mean + 1e-06) + 0.1)

        def scaled(step, carry):
            at = pl.ds(multiple(step * strip, strip), strip)
            cot = total[clip, at, :] * factor
            grad_proj[pl.ds(multiple(clip * length + step * strip, strip), strip), :] = (
                coef[clip, 2:3, :] * cot
            ).astype(half)
            return carry

        lax.fori_loop(0, length // strip, scaled, 0)

    def grad_copies(clip, part):
        result = []
        for slot in range(3):
            at = pl.ds(multiple(part * chunk, 128), chunk)
            out_at = pl.ds(multiple(slot * att + me * att_dev + part * chunk, 128), chunk)
            result.append(
                (
                    pltpu.make_async_remote_copy(
                        src_ref=grads.at[clip, slot, pl.ds(multiple(other * len_dev, 64), len_dev), at],
                        dst_ref=d_qkv.at[clip, :, out_at],
                        send_sem=grad_send.at[clip, part, slot],
                        recv_sem=grad_recv.at[clip, part, slot],
                        device_id={"seq": other},
                        device_id_type=MESH,
                    ),
                    pltpu.make_async_copy(
                        grads.at[clip, slot, pl.ds(multiple(me * len_dev, 64), len_dev), at],
                        d_qkv.at[clip, :, out_at],
                        grad_own.at[clip, part, slot],
                    ),
                )
            )
        return result

    def attend_back(clip, part):
        cosine, sine = cos_tab[clip], sin_tab[clip]
        grad_att = dot(
            grad_proj[pl.ds(multiple(clip * length, length), length), :],
            weight[pl.ds(multiple(part * chunk, 128), chunk), :],
            1,
            1,
        ).astype(half)
        for head in range(chunk // HEAD_DIM):
            at = pl.ds(multiple(part * chunk + head * HEAD_DIM, 128), HEAD_DIM)
            query, key, value = arrived[clip, 0, :, at], arrived[clip, 1, :, at], arrived[clip, 2, :, at]
            upper = grad_att[:, head * HEAD_DIM : (head + 1) * HEAD_DIM]
            probs = softmax_rows(dot(query, key, 1, 1) * scale)
            grad_value = dot(probs.astype(half), upper, 0, 0).astype(half)
            grad_prob = dot(upper, value, 1, 1)
            grad_score = (
                probs * (grad_prob - jnp.sum(probs * grad_prob, axis=-1, keepdims=True)) * scale
            ).astype(half)
            grad_query = dot(grad_score, key, 1, 0).astype(half)
            grad_key = dot(grad_score, query, 0, 0).astype(half)
            grads[clip, 0, :, at] = turn(grad_query, cosine, -sine)
            grads[clip, 1, :, at] = turn(grad_key, cosine, -sine)
            grads[clip, 2, :, at] = grad_value
        for remote, own in grad_copies(clip, part):
            remote.start()
            own.start()

    def back(clip):
        def step(part, carry):
            attend_back(clip, part)
            return carry

        lax.fori_loop(0, chunks, step, 0)

    def to_core(step, at_column):
        to_plane = (plane + 1 + step) % PLANES
        return pltpu.make_async_remote_copy(
            src_ref=partial.at[block_at(to_plane, at_column, 1 - core), :],
            dst_ref=from_core.at[step, at_column],
            send_sem=core_send.at[step, at_column],
            recv_sem=core_recv.at[step, at_column],
            device_id={"dp": index(plane, column, 1 - core)},
            device_id_type=MESH,
        )

    def to_column(step):
        to_plane = (plane + 1 + step) % PLANES
        return pltpu.make_async_remote_copy(
            src_ref=partial.at[block_at(to_plane, 1 - column, core), :],
            dst_ref=from_column.at[step],
            send_sem=column_send.at[step],
            recv_sem=column_recv.at[step],
            device_id={"dp": index(plane, 1 - column, core)},
            device_id_type=MESH,
        )

    def to_plane_copy(step):
        to_plane = (plane + 1 + step) % PLANES
        return pltpu.make_async_remote_copy(
            src_ref=partial.at[block_at(to_plane, column, core), :],
            dst_ref=from_plane.at[step],
            send_sem=plane_send.at[step],
            recv_sem=plane_recv.at[step],
            device_id={"dp": index(to_plane, column, core)},
            device_id_type=MESH,
        )

    piece = COLUMNS * CORES * block

    def weight_piece(step, carry):
        to_plane = (plane + 1 + step) % PLANES
        cols = pl.ds(multiple(to_plane * piece, 128), piece)
        left = jnp.concatenate([rows[clip, :length, cols] for clip in range(clips)], 0)

        def one(part, inner):
            at = pl.ds(multiple(part * tile, 128), tile)
            partial[pl.ds(multiple(to_plane * piece, 128), piece), at] = dot(
                left, grad_proj[:, at], 0, 0
            ).astype(half)
            return inner

        lax.fori_loop(0, tiles, one, 0)
        to_core(step, 0).start()
        to_core(step, 1).start()
        return carry

    def add_rows(row, source):
        for lower in range(0, block, 32):
            at = pl.ds(multiple(row * block + lower, 32), 32)
            partial[at, :] = (
                partial[at, :].astype(f32) + source[lower : lower + 32, :].astype(f32)
            ).astype(half)

    def core_stage(step, carry):
        to_plane = (plane + 1 + step) % PLANES
        to_core(step, 0).wait()
        to_core(step, 1).wait()
        for at_column in range(COLUMNS):
            add_rows(index(to_plane, at_column, core), from_core.at[step, at_column])
        to_column(step).start()
        return carry

    def column_stage(step):
        to_plane = (plane + 1 + step) % PLANES
        to_column(step).wait()
        add_rows(index(to_plane, column, core), from_column.at[step])

    def send_plane(step, carry):
        column_stage(step)
        to_plane_copy(step).start()
        return carry

    differentiate(0)
    back(0)
    for clip in range(1, clips):
        differentiate(clip)
    lax.fori_loop(0, PLANES, weight_piece, 0)
    lax.fori_loop(0, PLANES, core_stage, 0)
    for clip in range(1, clips):
        for part in range(chunks):
            attend_back(clip, part)
            if clip == 1:
                send_plane(part, 0)
    column_stage(PLANES - 1)
    for step in range(PLANES - 1):
        to_plane_copy(step).wait()
    root = 1.0 / math.sqrt(token_count)
    for lower in range(0, block, 32):
        own = multiple(index(plane, column, core) * block + lower, 32)
        value = partial[pl.ds(own, 32), :].astype(f32)
        for step in range(PLANES - 1):
            value = value + from_plane[step, lower : lower + 32, :].astype(f32)
        d_weight[lower : lower + 32, :] = value * root

    def finish(step, carry):
        for remote, own in grad_copies(step // chunks, step % chunks):
            remote.wait()
            own.wait()
        return carry

    lax.fori_loop(0, clips * chunks, finish, 0)


def whole_positions(positions, seq_len, len_dev):
    first = (positions[0, :, 0] * GRID_H + positions[1, :, 0]) * GRID_W + positions[2, :, 0]
    first = first - lax.axis_index("seq") * len_dev
    token = first[:, None] + jnp.arange(seq_len, dtype=jnp.int32)[None, :]
    rest = token % (GRID_H * GRID_W)
    return jnp.stack([token // (GRID_H * GRID_W), rest // GRID_W, rest % GRID_W])


def body_pair(
    qkv,
    qkv_tan,
    positions,
    step_index,
    resid,
    resid_tan,
    noisy,
    noisy_tan,
    out_weight,
    gate_bias,
    gate_amp,
    gate_freq,
):
    f32, half = jnp.float32, jnp.bfloat16
    clips, len_dev, triple = qkv.shape
    att_dev = triple // 6
    seq_len = len_dev * 2
    width = resid.shape[2]
    block = out_weight.shape[0]
    angle = rope_angles(whole_positions(positions, seq_len, len_dev))
    angle = jnp.concatenate([angle, angle], -1)
    vmem = pl.BlockSpec(memory_space=pltpu.VMEM)
    hbm = pl.BlockSpec(memory_space=pl.ANY)
    chunks = 3
    dma = pltpu.SemaphoreType.DMA
    time = 0.05 + 1.47 * (step_index.astype(f32) + 0.5) / NT
    phase = gate_freq[None, :] * time[:, None]
    gate = gate_bias + gate_amp * jnp.sin(phase)
    slope = gate_amp * gate_freq * jnp.cos(phase)
    cos_sq = (jnp.cos(time) ** 2)[:, None]
    cross = (jnp.cos(time) * jnp.sin(time))[:, None]
    known = -cos_sq[:, :, None] * (0.5 * resid.astype(f32) - noisy_tan.astype(f32)) - cross[
        :, :, None
    ] * (noisy.astype(f32) + 0.5 * resid_tan.astype(f32))
    coef = jnp.stack(
        [-0.5 * (cos_sq * gate + cross * slope), -0.5 * cross * gate, gate], axis=1
    )
    tiles = 5
    return pl.pallas_call(
        step_kernel,
        out_shape=(
            jax.ShapeDtypeStruct((clips, len_dev, triple), half),
            jax.ShapeDtypeStruct((block, width), f32),
        ),
        in_specs=[hbm, hbm, vmem, vmem, vmem, vmem],
        out_specs=(hbm, vmem),
        scratch_shapes=[
            pltpu.VMEM((clips, 6, seq_len, att_dev), half),
            pltpu.VMEM((clips, 2 * seq_len, att_dev), half),
            pltpu.VMEM((clips, seq_len, HEAD_DIM), f32),
            pltpu.VMEM((clips, seq_len, HEAD_DIM), f32),
            pltpu.VMEM((att_dev, width), half),
            pltpu.VMEM((clips, seq_len, width), f32),
            pltpu.VMEM((clips, seq_len, width), half),
            pltpu.VMEM((clips, seq_len, width), half),
            pltpu.VMEM((clips * seq_len, width), half),
            pltpu.VMEM((clips, 3, seq_len, att_dev), half),
            pltpu.VMEM((att_dev, width), half),
            pltpu.VMEM((PLANES, COLUMNS, block, width), half),
            pltpu.VMEM((PLANES, block, width), half),
            pltpu.VMEM((PLANES - 1, block, width), half),
            dma((clips, chunks, 6)),
            dma((clips, chunks, 6)),
            dma((clips, chunks, 6)),
            dma((4 * PLANES - 1,)),
            dma((4 * PLANES - 1,)),
            dma((clips, tiles)),
            dma((clips, tiles)),
            dma((clips, chunks, 3)),
            dma((clips, chunks, 3)),
            dma((clips, chunks, 3)),
            dma((PLANES, COLUMNS)),
            dma((PLANES, COLUMNS)),
            dma((PLANES,)),
            dma((PLANES,)),
            dma((PLANES - 1,)),
            dma((PLANES - 1,)),
        ],
        compiler_params=pltpu.CompilerParams(
            collective_id=0, has_side_effects=True, vmem_limit_bytes=58 * 2**20
        ),
    )(qkv, qkv_tan, angle, out_weight, known, coef)


def solution(mesh):
    placed = (
        P("dp", "seq", None),
        P("dp", "seq", None),
        P(None, "dp", "seq"),
        P("dp"),
        P("dp", "seq", None),
        P("dp", "seq", None),
        P("dp", "seq", None),
        P("dp", "seq", None),
        P(("seq", "dp"), None),
        P(),
        P(),
        P(),
    )
    fits = mesh.shape["dp"] == PLANES * COLUMNS * CORES and mesh.shape["seq"] == 2
    return jax.shard_map(
        body_pair if fits else body,
        mesh=mesh,
        in_specs=placed,
        out_specs=(P("dp", "seq", None), P(("seq", "dp"), None)),
        check_vma=False,
    )
```
